32 devices in a mesh: dp: 4 (over z), tensor: 8 (over y, x, core).
Axes of the slice: x: 2, y: 2, z: 4, core: 2. Of those that a mesh axis runs over, the one named last changes fastest.
Arguments:
- tokens: bfloat16 [2048, 2304], P(('dp', 'tensor')), may hold values from -6 to 6
- cotangent: bfloat16 [2048, 2304], P(('dp', 'tensor')), may hold values from -20 to 20
- gate_weight: bfloat16 [2304, 18432], P(None, 'tensor'), may hold values from -0.125 to 0.125
- up_weight: bfloat16 [2304, 18432], P(None, 'tensor'), may hold values from -0.1875 to 0.1875
- down_weight: bfloat16 [18432, 2304], P('tensor'), may hold values from -0.046875 to 0.046875
Outputs:
- input_grad: bfloat16 [2048, 2304], P(('dp', 'tensor'))
- grad_gate: float32 [2304, 18432], P('dp', 'tensor')
- grad_up: float32 [2304, 18432], P('dp', 'tensor')
- grad_down: float32 [18432, 2304], P('tensor', 'dp')
The draws below stay inside these ranges and needn't reach their ends.
All inputs are finite; a program needn't handle non-finite values.
Results may differ from the reference program's by a relative error of at most 0.017.
Values may be sent and summed in bfloat16 or wider, within the bound.
A program may use at most 256 MiB of HBM per device.

```python
import math
import jax
import jax.numpy as jnp
from jax import lax

D = 2304
FF = 18432
SEQ = 256
TOKENS = 2048


def draw_tokens(key, part):
    key = jax.random.fold_in(key, 13)
    entry_key = jax.random.fold_in(key, 0)
    base = jnp.clip(jax.random.normal(entry_key, (TOKENS, D), jnp.float32), -6.0, 6.0)
    return base.astype(jnp.bfloat16)


def draw_cotangent(key, part):
    key = jax.random.fold_in(key, 11)
    level_key, entry_key = jax.random.split(key)
    levels = jnp.exp(jax.random.uniform(level_key, (TOKENS // SEQ,), jnp.float32, jnp.log(0.25), jnp.log(4.0)))
    base = jnp.clip(jax.random.normal(entry_key, (TOKENS, D), jnp.float32), -5.0, 5.0)
    row_levels = jnp.repeat(levels, SEQ)
    return (base * row_levels[:, None]).astype(jnp.bfloat16)


def draw_up_weight(key, part):
    key = jax.random.fold_in(key, 12)
    ramp = 0.6 * 3.0 ** (jnp.arange(FF, dtype=jnp.float32) / FF)
    base = jnp.clip(jax.random.normal(key, (D, FF), jnp.float32), -5.0, 5.0)
    return (base * ramp[None, :] / jnp.sqrt(jnp.float32(D))).astype(jnp.bfloat16)


def block_scale(own_key, shape, cuts, low, largest):
    level, own = 1.0, jax.random.fold_in(own_key, 6)
    for axis_at, blocks in cuts:
        steps = jnp.exp(jax.random.uniform(jax.random.fold_in(own, axis_at), (blocks,), jnp.float32, low / len(cuts), largest / len(cuts)))
        level = level * jnp.repeat(steps, shape[axis_at] // blocks).reshape([-1 if axis == axis_at else 1 for axis in range(len(shape))])
    return level


def bell_draw(own_key, extent, width, bound, shards=(), kind=jnp.bfloat16):
    result = width * jax.random.normal(own_key, extent, jnp.float32)
    if shards:
        result = result * block_scale(own_key, extent, shards, -0.22, 0.18)
    return jnp.clip(result, -bound, bound).astype(kind)


def setup_inputs(seed: int = 0) -> dict:
    arg_keys = jax.random.split(jax.random.key(seed), 6)
    return {
        "tokens": draw_tokens(jax.random.fold_in(arg_keys[5], 71), 0),
        "cotangent": draw_cotangent(jax.random.fold_in(arg_keys[5], 71), 0),
        "gate_weight": bell_draw(arg_keys[2], (D, FF), D ** -0.5, 0.125, ((1, 8),)),
        "up_weight": draw_up_weight(jax.random.fold_in(arg_keys[5], 71), 0),
        "down_weight": bell_draw(arg_keys[4], (FF, D), FF ** -0.5, 0.046875, ((0, 8),)),
    }


GELU_ROOT = math.sqrt(2.0 / math.pi)
GELU_CUBIC = 0.044715

def gelu_pair(value):
    inner = GELU_ROOT * (value + GELU_CUBIC * value * value * value)
    tangent = jnp.tanh(inner)
    activ = 0.5 * value * (1.0 + tangent)
    slope = 0.5 * (1.0 + tangent) + 0.5 * value * (1.0 - tangent * tangent) * GELU_ROOT * (1.0 + 3.0 * GELU_CUBIC * value * value)
    return (activ, slope)

def reference(tokens, cotangent, gate_weight, up_weight, down_weight):
    pre_gate = jnp.dot(tokens, gate_weight, preferred_element_type=jnp.float32)
    pre_up = jnp.dot(tokens, up_weight, preferred_element_type=jnp.float32)
    activ, slope = gelu_pair(pre_gate)
    hidden = (activ * pre_up).astype(jnp.bfloat16)
    grad_hidden = jnp.dot(cotangent, down_weight.T, preferred_element_type=jnp.float32)
    grad_pre_gate = (grad_hidden * pre_up * slope).astype(jnp.bfloat16)
    grad_pre_up = (grad_hidden * activ).astype(jnp.bfloat16)
    input_grad = (jnp.dot(grad_pre_gate, gate_weight.T, preferred_element_type=jnp.float32) + jnp.dot(grad_pre_up, up_weight.T, preferred_element_type=jnp.float32)).astype(jnp.bfloat16)
    total = TOKENS // SEQ
    inputs_ex = tokens.reshape(total, SEQ, D).astype(jnp.float32)
    cotan_ex = cotangent.reshape(total, SEQ, D).astype(jnp.float32)
    gate_ex = grad_pre_gate.reshape(total, SEQ, FF).astype(jnp.float32)
    up_ex = grad_pre_up.reshape(total, SEQ, FF).astype(jnp.float32)
    hidden_ex = hidden.reshape(total, SEQ, FF).astype(jnp.float32)
    gram_in = jnp.einsum('esd,etd->est', inputs_ex, inputs_ex)
    gram_cot = jnp.einsum('esd,etd->est', cotan_ex, cotan_ex)
    gram_gate = jnp.einsum('esf,etf->est', gate_ex, gate_ex)
    gram_up = jnp.einsum('esf,etf->est', up_ex, up_ex)
    gram_hid = jnp.einsum('esf,etf->est', hidden_ex, hidden_ex)
    norm_sq = lax.optimization_barrier(jnp.sum(gram_in * (gram_gate + gram_up) + gram_hid * gram_cot, axis=(1, 2)))
    clip_level = math.sqrt(SEQ * D * (FF // 2 + D))
    factor = math.sqrt(D * FF) / jnp.maximum(clip_level, jnp.sqrt(norm_sq))

    def accumulate(carry, pieces):
        inputs_one, cotan_one, gate_one, up_one, hidden_one, scale = pieces
        new_gate = carry[0] + scale * jnp.dot(inputs_one.T, gate_one, preferred_element_type=jnp.float32)
        new_up = carry[1] + scale * jnp.dot(inputs_one.T, up_one, preferred_element_type=jnp.float32)
        new_down = carry[2] + scale * jnp.dot(hidden_one.T, cotan_one, preferred_element_type=jnp.float32)
        return ((new_gate, new_up, new_down), None)
    start_sums = (jnp.zeros((D, FF), jnp.float32), jnp.zeros((D, FF), jnp.float32), jnp.zeros((FF, D), jnp.float32))
    pieces = (tokens.reshape(total, SEQ, D), cotangent.reshape(total, SEQ, D), grad_pre_gate.reshape(total, SEQ, FF), grad_pre_up.reshape(total, SEQ, FF), hidden.reshape(total, SEQ, FF), factor)
    sums, unused = lax.scan(accumulate, start_sums, pieces)
    return (input_grad, sums[0], sums[1], sums[2])
```

```python
import functools
import math

import jax
import jax.numpy as jnp
from jax import lax
from jax.experimental import pallas as pl
from jax.experimental.pallas import tpu as pltpu
from jax.sharding import PartitionSpec as P

D = 2304
FF = 18432
SEQ = 256
MESH = pl.DeviceIdType.MESH

GELU_ROOT = math.sqrt(2.0 / math.pi)
GELU_CUBIC = 0.044715


def gelu_pair(value):
    square = value * value
    inner = GELU_ROOT * (value + GELU_CUBIC * (square * value))
    tangent = jnp.tanh(inner)
    half = 0.5 * (1.0 + tangent)
    activ = value * half
    slope = half + 0.5 * value * (1.0 - tangent * tangent) * (
        GELU_ROOT * (1.0 + 3.0 * GELU_CUBIC * square)
    )
    return (activ, slope)


def nt(a, b):
    return lax.dot_general(a, b, (((1,), (1,)), ((), ())), preferred_element_type=jnp.float32)


def kernel(
    planes, width, x, gw, uw, dw,
    gathered, out_gate, out_up, out_hid, norm_out, input_grad,
    gw_v, uw_v, dw_v, xb, ob, partial, landed, tiles, norms,
    w_sem, own_sem, x_sem, o_sem, z_send, z_recv, p_send, p_recv, s_send, s_recv,
    r_send, r_recv, n_send, n_recv, m_send, m_recv,
):
    z = lax.axis_index("dp")
    t = lax.axis_index("tensor")
    core = lax.rem(t, 2)
    sibling = t + 1 - 2 * core
    chips = width // 2
    rows = x.shape[1]
    many = rows * width
    units = gw.shape[1]
    step = 256 if units % 256 == 0 else units
    n_tiles = units // step
    outs = (out_gate, out_up, out_hid)

    def plane(j):
        return lax.rem(z + j, planes)

    def spot(j, owner):
        at = pl.multiple_of(owner * rows, rows)
        return gathered.at[:, plane(j), pl.ds(at, rows), :]

    def peer(k):
        return lax.rem(t + k, width)

    def to_z(j):
        return pltpu.make_async_remote_copy(
            src_ref=x, dst_ref=spot(0, t), send_sem=z_send.at[j], recv_sem=z_recv.at[j],
            device_id=(lax.rem(z + planes - j, planes), t), device_id_type=MESH)

    def from_z(j):
        return pltpu.make_async_remote_copy(
            src_ref=x, dst_ref=spot(j, t), send_sem=z_send.at[j], recv_sem=z_recv.at[j],
            device_id=(plane(j), t), device_id_type=MESH)

    def to_peer(j, k):
        return pltpu.make_async_remote_copy(
            src_ref=x if j == 0 else spot(j, t), dst_ref=spot(j, t),
            send_sem=p_send.at[j, k], recv_sem=p_recv.at[j, k],
            device_id=(z, peer(2 * k)), device_id_type=MESH)

    def from_peer(j, k):
        owner = peer(width - 2 * k)
        return pltpu.make_async_remote_copy(
            src_ref=x, dst_ref=spot(j, owner),
            send_sem=p_send.at[j, k], recv_sem=p_recv.at[j, k],
            device_id=(z, owner), device_id_type=MESH)

    def to_sibling(j, k):
        owner = peer(width - 2 * k) if k else t
        return pltpu.make_async_remote_copy(
            src_ref=x if j == 0 and k == 0 else spot(j, owner), dst_ref=spot(j, owner),
            send_sem=s_send.at[j, k], recv_sem=s_recv.at[j, k],
            device_id=(z, sibling), device_id_type=MESH)

    def from_sibling(j, k):
        owner = lax.rem(sibling + width - 2 * k, width)
        return pltpu.make_async_remote_copy(
            src_ref=x, dst_ref=spot(j, owner),
            send_sem=s_send.at[j, k], recv_sem=s_recv.at[j, k],
            device_id=(z, sibling), device_id_type=MESH)

    def spread(j):
        if j >= planes:
            return
        if j:
            from_z(j).wait_recv()
        for k in range(1, chips):
            to_peer(j, k).start()
        to_sibling(j, 0).start()

    def hand_on(j):
        if j >= planes:
            return
        for k in range(1, chips):
            from_peer(j, k).wait_recv()
            to_sibling(j, k).start()

    def load(j):
        return pltpu.make_async_copy(gathered.at[:, plane(j)], xb.at[j % 2], x_sem.at[j % 2])

    def fetch(j):
        if j >= planes:
            return
        for k in range(chips):
            from_sibling(j, k).wait_recv()
        if j == 0:
            own.wait()
        load(j).start()

    weights = [
        pltpu.make_async_copy(src, dst, w_sem.at[i])
        for i, (src, dst) in enumerate(((gw, gw_v), (uw, uw_v), (dw, dw_v)))
    ]
    own = pltpu.make_async_copy(x, spot(0, t), own_sem)

    barrier = pltpu.get_barrier_semaphore()
    for k in range(1, width):
        pl.semaphore_signal(barrier, inc=1, device_id=(z, peer(k)), device_id_type=MESH)
    for j in range(1, planes):
        pl.semaphore_signal(barrier, inc=1, device_id=(plane(j), t), device_id_type=MESH)
    pl.semaphore_wait(barrier, width + planes - 2)

    spread(0)
    for j in range(1, planes):
        to_z(j).start()
    own.start()
    for copy in weights:
        copy.start()

    def out_copies(j, n, cols):
        return [
            pltpu.make_async_copy(
                ob.at[i, :, cols], outs[i].at[plane(j), :, cols], o_sem.at[i, n])
            for i in range(3)
        ]

    def tile(j, n):
        if n_tiles == 1:
            cols = slice(None)
            lines = slice(None)
        else:
            at = pl.multiple_of(n * step, step)
            cols = pl.ds(at, step)
            lines = pl.ds(at, step)
        pre_gate = jnp.dot(xb[j % 2, 0], gw_v[:, cols], preferred_element_type=jnp.float32)
        activ, slope = gelu_pair(pre_gate)
        pre_up = jnp.dot(xb[j % 2, 0], uw_v[:, cols], preferred_element_type=jnp.float32)
        grad_hidden = nt(xb[j % 2, 1], dw_v[lines, :])
        if j:
            for copy in out_copies(j - 1, n, cols):
                copy.wait()
        ob[0, :, cols] = (grad_hidden * pre_up * slope).astype(jnp.bfloat16)
        ob[1, :, cols] = (grad_hidden * activ).astype(jnp.bfloat16)
        ob[2, :, cols] = (activ * pre_up).astype(jnp.bfloat16)
        for copy in out_copies(j, n, cols):
            copy.start()

    def part(j, third):
        low, high = n_tiles * third // 3, n_tiles * (third + 1) // 3
        if n_tiles == 1:
            if high > low:
                tile(j, 0)
        elif high > low:
            pl.loop(low, high)(functools.partial(tile, j))

    def send_tile(k):
        return pltpu.make_async_remote_copy(
            src_ref=tiles.at[t], dst_ref=tiles.at[t], send_sem=n_send.at[k],
            recv_sem=n_recv.at[k], device_id=(z, peer(k)), device_id_type=MESH)

    def take_tile(k):
        owner = peer(width - k)
        return pltpu.make_async_remote_copy(
            src_ref=tiles.at[t], dst_ref=tiles.at[owner], send_sem=n_send.at[k],
            recv_sem=n_recv.at[k], device_id=(z, owner), device_id_type=MESH)

    def send_norm(j):
        return pltpu.make_async_remote_copy(
            src_ref=norms.at[z], dst_ref=norms.at[z], send_sem=m_send.at[j],
            recv_sem=m_recv.at[j], device_id=(lax.rem(z + planes - j, planes), t),
            device_id_type=MESH)

    def take_norm(j):
        return pltpu.make_async_remote_copy(
            src_ref=norms.at[z], dst_ref=norms.at[plane(j)], send_sem=m_send.at[j],
            recv_sem=m_recv.at[j], device_id=(plane(j), t), device_id_type=MESH)

    def send_rows(k):
        to = peer(k)
        return pltpu.make_async_remote_copy(
            src_ref=partial.at[pl.ds(pl.multiple_of(to * rows, rows), rows), :],
            dst_ref=landed.at[k], send_sem=r_send.at[k], recv_sem=r_recv.at[k],
            device_id=(z, to), device_id_type=MESH)

    hand_on(0)
    fetch(0)
    spread(1)
    load(0).wait()
    for copy in weights:
        copy.wait()

    part(0, 0)
    spread(2)
    part(0, 1)
    part(0, 2)

    sums = []
    for e in range(many // SEQ):
        cut = slice(e * SEQ, (e + 1) * SEQ)
        tok, cot = xb[0, 0, cut, :], xb[0, 1, cut, :]
        gate, up, hid = ob[0, cut, :], ob[1, cut, :], ob[2, cut, :]
        terms = nt(tok, tok) * (nt(gate, gate) + nt(up, up)) + nt(hid, hid) * nt(cot, cot)
        sums.append(jnp.sum(jnp.sum(terms, axis=1, keepdims=True), axis=0, keepdims=True))
    line = lax.broadcasted_iota(jnp.int32, (8, 128), 0)
    board = jnp.zeros((8, 128), jnp.float32)
    for e, value in enumerate(sums):
        board = jnp.where(line == e, value, board)
    tiles[t] = board
    for k in range(1, width):
        send_tile(k).start()
    hand_on(1)

    @pl.loop(0, D // 256)
    def _(d):
        lines = pl.ds(pl.multiple_of(d * 256, 256), 256)
        total = nt(ob[0], gw_v[lines, :]) + nt(ob[1], uw_v[lines, :])
        partial[:, lines] = total.astype(jnp.bfloat16)

    for k in range(1, width):
        send_rows(k).start()
    fetch(1)

    for j in range(1, planes):
        spread(j + 2)
        load(j).wait()
        part(j, 0)
        if j == 1:
            for k in range(1, width):
                take_tile(k).wait_recv()
            norms[z] = jnp.sum(tiles[...], axis=0)
            for i in range(1, planes):
                send_norm(i).start()
        hand_on(j + 1)
        part(j, 1)
        fetch(j + 1)
        part(j, 2)

    mine = pl.ds(pl.multiple_of(t * rows, rows), rows)
    total = partial[mine, :].astype(jnp.float32)
    for k in range(1, width):
        send_rows(k).wait_recv()
        total = total + landed[k].astype(jnp.float32)
    input_grad[...] = total.astype(jnp.bfloat16)
    for i in range(1, planes):
        take_norm(i).wait_recv()
    norm_out[...] = norms[...]

    for j in range(1, planes):
        to_z(j).wait_send()
        send_norm(j).wait_send()
    for k in range(1, width):
        send_tile(k).wait_send()
        send_rows(k).wait_send()
    for j in range(planes):
        for k in range(1, chips):
            to_peer(j, k).wait_send()
        for k in range(chips):
            to_sibling(j, k).wait_send()
    if n_tiles == 1:
        for copy in out_copies(planes - 1, 0, slice(None)):
            copy.wait()
    else:
        @pl.loop(0, n_tiles)
        def _(n):
            for copy in out_copies(planes - 1, n, pl.ds(pl.multiple_of(n * step, step), step)):
                copy.wait()


def body(planes, width, tokens, cotangent, gate_weight, up_weight, down_weight):
    rows, units = tokens.shape[0], gate_weight.shape[1]
    many, chips = rows * width, width // 2
    tiles = units // 256 if units % 256 == 0 else 1
    half = jnp.bfloat16
    anywhere = pl.BlockSpec(memory_space=pl.ANY)
    inside = pl.BlockSpec(memory_space=pltpu.VMEM)
    dma = pltpu.SemaphoreType.DMA
    produced = jax.ShapeDtypeStruct((planes, many, units), half)
    gathered, gate, up, hidden, norms, input_grad = pl.pallas_call(
        functools.partial(kernel, planes, width),
        out_shape=(
            jax.ShapeDtypeStruct((2, planes, many, D), half),
            produced, produced, produced,
            jax.ShapeDtypeStruct((planes, 8, 128), jnp.float32),
            jax.ShapeDtypeStruct((rows, D), half),
        ),
        in_specs=[anywhere] * 4,
        out_specs=(anywhere,) * 4 + (inside,) * 2,
        scratch_shapes=[
            pltpu.VMEM((D, units), half),
            pltpu.VMEM((D, units), half),
            pltpu.VMEM((units, D), half),
            pltpu.VMEM((2, 2, many, D), half),
            pltpu.VMEM((3, many, units), half),
            pltpu.VMEM((many, D), half),
            pltpu.VMEM((width, rows, D), half),
            pltpu.VMEM((width, 8, 128), jnp.float32),
            pltpu.VMEM((planes, 8, 128), jnp.float32),
            dma((3,)), dma, dma((2,)), dma((3, tiles)),
            dma((planes,)), dma((planes,)),
            dma((planes, chips)), dma((planes, chips)),
            dma((planes, chips)), dma((planes, chips)),
            dma((width,)), dma((width,)),
            dma((width,)), dma((width,)),
            dma((planes,)), dma((planes,)),
        ],
        compiler_params=pltpu.CompilerParams(
            collective_id=0, has_side_effects=True, vmem_limit_bytes=63 * 1024 * 1024
        ),
    )(jnp.stack([tokens, cotangent]), gate_weight, up_weight, down_weight)

    examples = many // SEQ
    norm_sq = norms[:, :examples, 0].reshape(planes * examples)
    clip_level = math.sqrt(SEQ * D * (FF // 2 + D))
    factor = math.sqrt(D * FF) / jnp.maximum(clip_level, jnp.sqrt(norm_sq))
    scale = jnp.repeat(factor, SEQ).reshape(1, planes * many, 1)
    share = D // planes
    cut = lax.dynamic_slice_in_dim(
        gathered.reshape(2, planes * many, D), lax.axis_index("dp") * share, share, axis=2)
    scaled = (cut.astype(jnp.float32) * scale).astype(half)

    def first(a, b):
        return lax.dot_general(a, b, (((0,), (0,)), ((), ())), preferred_element_type=jnp.float32)

    grad_gate = first(scaled[0], gate.reshape(planes * many, units))
    grad_up = first(scaled[0], up.reshape(planes * many, units))
    grad_down = first(hidden.reshape(planes * many, units), scaled[1])
    return (input_grad, grad_gate, grad_up, grad_down)


def solution(mesh):
    placed = (
        P(("dp", "tensor"), None),
        P(("dp", "tensor"), None),
        P(None, "tensor"),
        P(None, "tensor"),
        P("tensor", None),
    )
    return jax.shard_map(
        functools.partial(body, mesh.shape["dp"], mesh.shape["tensor"]),
        mesh=mesh,
        in_specs=placed,
        out_specs=(
            P(("dp", "tensor"), None),
            P("dp", "tensor"),
            P("dp", "tensor"),
            P("tensor", "dp"),
        ),
        check_vma=False,
    )
```

```python
import functools
import math

import jax
import jax.numpy as jnp
from jax import lax
from jax.experimental import pallas as pl
from jax.experimental.pallas import tpu as pltpu
from jax.sharding import PartitionSpec as P

D = 2304
FF = 18432
SEQ = 256
MESH = pl.DeviceIdType.MESH

GELU_ROOT = math.sqrt(2.0 / math.pi)
GELU_CUBIC = 0.044715


def gelu_pair(value):
    square = value * value
    inner = GELU_ROOT * (value + GELU_CUBIC * (square * value))
    tangent = jnp.tanh(inner)
    half = 0.5 * (1.0 + tangent)
    activ = value * half
    slope = half + 0.5 * value * (1.0 - tangent * tangent) * (
        GELU_ROOT * (1.0 + 3.0 * GELU_CUBIC * square)
    )
    return (activ, slope)


def nt(a, b):
    return lax.dot_general(a, b, (((1,), (1,)), ((), ())), preferred_element_type=jnp.float32)


def kernel(
    planes, width, x, gw, uw, dw,
    gathered, out_gate, out_up, out_hid, scaled_in, scaled_cot, input_grad,
    gw_v, uw_v, dw_v, xb, ob, partial, landed, tiles, norms,
    w_sem, own_sem, x_sem, o_sem, z_send, z_recv, p_send, p_recv, s_send, s_recv,
    r_send, r_recv, n_send, n_recv, m_send, m_recv, q_send, q_recv,
):
    z = lax.axis_index("dp")
    t = lax.axis_index("tensor")
    core = lax.rem(t, 2)
    sibling = t + 1 - 2 * core
    chips = width // 2
    rows = x.shape[1]
    many = rows * width
    units = gw.shape[1]
    step = 256 if units % 256 == 0 else units
    n_tiles = units // step
    outs = (out_gate, out_up, out_hid)
    scaled = (scaled_in, scaled_cot)

    def plane(j):
        return lax.rem(z + j, planes)

    def spot(j, owner):
        at = pl.multiple_of(owner * rows, rows)
        return gathered.at[:, plane(j), pl.ds(at, rows), :]

    def peer(k):
        return lax.rem(t + k, width)

    def to_z(j):
        return pltpu.make_async_remote_copy(
            src_ref=x, dst_ref=spot(0, t), send_sem=z_send.at[j], recv_sem=z_recv.at[j],
            device_id=(lax.rem(z + planes - j, planes), t), device_id_type=MESH)

    def from_z(j):
        return pltpu.make_async_remote_copy(
            src_ref=x, dst_ref=spot(j, t), send_sem=z_send.at[j], recv_sem=z_recv.at[j],
            device_id=(plane(j), t), device_id_type=MESH)

    folded = chips == 4
    direct = range(1, 3) if folded else range(1, chips)

    def owner_at(k, side):
        if not folded:
            return lax.rem(side + width - 2 * k, width)
        chip = side // 2
        low, high = lax.rem(chip, 2), chip // 2
        if k % 2:
            low = 1 - low
        if k // 2:
            high = 1 - high
        return (2 * high + low) * 2 + lax.rem(side, 2)

    def to_peer(j, k):
        return pltpu.make_async_remote_copy(
            src_ref=x if j == 0 else spot(j, t), dst_ref=spot(j, t),
            send_sem=p_send.at[j, k], recv_sem=p_recv.at[j, k],
            device_id=(z, owner_at(k, t) if folded else peer(2 * k)), device_id_type=MESH)

    def from_peer(j, k):
        owner = owner_at(k, t)
        return pltpu.make_async_remote_copy(
            src_ref=x, dst_ref=spot(j, owner),
            send_sem=p_send.at[j, k], recv_sem=p_recv.at[j, k],
            device_id=(z, owner), device_id_type=MESH)

    def to_across(j, f):
        block = spot(j, owner_at(2 - f, t)).at[f]
        return pltpu.make_async_remote_copy(
            src_ref=block, dst_ref=block,
            send_sem=q_send.at[j, f], recv_sem=q_recv.at[j, f],
            device_id=(z, owner_at(1 + f, t)), device_id_type=MESH)

    def from_across(j, f):
        block = spot(j, owner_at(3, t)).at[f]
        return pltpu.make_async_remote_copy(
            src_ref=x.at[f], dst_ref=block,
            send_sem=q_send.at[j, f], recv_sem=q_recv.at[j, f],
            device_id=(z, owner_at(1 + f, t)), device_id_type=MESH)

    def to_sibling(j, k):
        owner = owner_at(k, t) if k else t
        return pltpu.make_async_remote_copy(
            src_ref=x if j == 0 and k == 0 else spot(j, owner), dst_ref=spot(j, owner),
            send_sem=s_send.at[j, k], recv_sem=s_recv.at[j, k],
            device_id=(z, sibling), device_id_type=MESH)

    def from_sibling(j, k):
        owner = owner_at(k, sibling) if k else sibling
        return pltpu.make_async_remote_copy(
            src_ref=x, dst_ref=spot(j, owner),
            send_sem=s_send.at[j, k], recv_sem=s_recv.at[j, k],
            device_id=(z, sibling), device_id_type=MESH)

    def spread(j):
        if j >= planes:
            return
        if j:
            from_z(j).wait_recv()
        for k in direct:
            to_peer(j, k).start()
        to_sibling(j, 0).start()

    def hand_on(j):
        if j >= planes:
            return
        for k in direct:
            from_peer(j, k).wait_recv()
            if folded:
                to_across(j, 2 - k).start()
            to_sibling(j, k).start()

    def hand_across(j):
        if j >= planes or not folded:
            return
        for f in range(2):
            from_across(j, f).wait_recv()
        to_sibling(j, 3).start()

    def load(j):
        return pltpu.make_async_copy(gathered.at[:, plane(j)], xb.at[j % 2], x_sem.at[j % 2])

    def fetch(j):
        if j >= planes:
            return
        for k in range(chips):
            from_sibling(j, k).wait_recv()
        if j == 0:
            own.wait()
        load(j).start()

    weights = [
        pltpu.make_async_copy(src, dst, w_sem.at[i])
        for i, (src, dst) in enumerate(((gw, gw_v), (uw, uw_v), (dw, dw_v)))
    ]
    own = pltpu.make_async_copy(x, spot(0, t), own_sem)

    barrier = pltpu.get_barrier_semaphore()
    for k in range(1, width):
        pl.semaphore_signal(barrier, inc=1, device_id=(z, peer(k)), device_id_type=MESH)
    for j in range(1, planes):
        pl.semaphore_signal(barrier, inc=1, device_id=(plane(j), t), device_id_type=MESH)
    pl.semaphore_wait(barrier, width + planes - 2)

    spread(0)
    to_z(1).start()
    own.start()
    for copy in weights:
        copy.start()

    def out_copies(j, n, cols):
        return [
            pltpu.make_async_copy(
                ob.at[i, :, cols], outs[i].at[plane(j), :, cols], o_sem.at[i, n])
            for i in range(3)
        ]

    def tile(j, n):
        if n_tiles == 1:
            cols = slice(None)
            lines = slice(None)
        else:
            at = pl.multiple_of(n * step, step)
            cols = pl.ds(at, step)
            lines = pl.ds(at, step)
        if j:
            for copy in out_copies(j - 1, n, cols):
                copy.wait()
        pre_gate = jnp.dot(xb[j % 2, 0], gw_v[:, cols], preferred_element_type=jnp.float32)
        activ, slope = gelu_pair(pre_gate)
        pre_up = jnp.dot(xb[j % 2, 0], uw_v[:, cols], preferred_element_type=jnp.float32)
        grad_hidden = nt(xb[j % 2, 1], dw_v[lines, :])
        ob[0, :, cols] = (grad_hidden * pre_up * slope).astype(jnp.bfloat16)
        ob[1, :, cols] = (grad_hidden * activ).astype(jnp.bfloat16)
        ob[2, :, cols] = (activ * pre_up).astype(jnp.bfloat16)
        for copy in out_copies(j, n, cols):
            copy.start()

    def part(j, q):
        low, high = n_tiles * q // 4, n_tiles * (q + 1) // 4
        if n_tiles == 1:
            if high > low:
                tile(j, 0)
        elif high > low:
            pl.loop(low, high)(functools.partial(tile, j))

    share = D // planes
    shifts = sorted({share * i % 128 for i in range(planes)})
    window = -(-(share + shifts[-1]) // 128) * 128

    def cut(j):
        first = z * share
        lag = lax.rem(first, 128)
        for a in range(2):
            wide = xb[j % 2, a, :, pl.ds(pl.multiple_of(first - lag, 128), window)]
            part_of = wide[:, :share]
            for shift in shifts[1:]:
                part_of = jnp.where(lag == shift, wide[:, shift : shift + share], part_of)
            scaled[a][plane(j)] = part_of

    def send_tile(k):
        return pltpu.make_async_remote_copy(
            src_ref=tiles.at[t], dst_ref=tiles.at[t], send_sem=n_send.at[k],
            recv_sem=n_recv.at[k], device_id=(z, peer(k)), device_id_type=MESH)

    def take_tile(k):
        owner = peer(width - k)
        return pltpu.make_async_remote_copy(
            src_ref=tiles.at[t], dst_ref=tiles.at[owner], send_sem=n_send.at[k],
            recv_sem=n_recv.at[k], device_id=(z, owner), device_id_type=MESH)

    def send_norm(j):
        return pltpu.make_async_remote_copy(
            src_ref=norms.at[z], dst_ref=norms.at[z], send_sem=m_send.at[j],
            recv_sem=m_recv.at[j], device_id=(lax.rem(z + planes - j, planes), t),
            device_id_type=MESH)

    def take_norm(j):
        return pltpu.make_async_remote_copy(
            src_ref=norms.at[z], dst_ref=norms.at[plane(j)], send_sem=m_send.at[j],
            recv_sem=m_recv.at[j], device_id=(plane(j), t), device_id_type=MESH)

    def send_rows(k):
        to = peer(k)
        return pltpu.make_async_remote_copy(
            src_ref=partial.at[pl.ds(pl.multiple_of(to * rows, rows), rows), :],
            dst_ref=landed.at[k], send_sem=r_send.at[k], recv_sem=r_recv.at[k],
            device_id=(z, to), device_id_type=MESH)

    hand_on(0)
    for j in range(2, planes):
        to_z(j).start()
    hand_across(0)
    spread(1)
    fetch(0)
    load(0).wait()
    for copy in weights:
        copy.wait()

    part(0, 0)
    part(0, 1)
    spread(2)
    part(0, 2)
    hand_on(1)
    part(0, 3)
    hand_across(1)

    cut(0)
    sums = []
    for e in range(many // SEQ):
        at = slice(e * SEQ, (e + 1) * SEQ)
        tok, cot = xb[0, 0, at, :], xb[0, 1, at, :]
        gate, up, hid = ob[0, at, :], ob[1, at, :], ob[2, at, :]
        terms = nt(tok, tok) * (nt(gate, gate) + nt(up, up)) + nt(hid, hid) * nt(cot, cot)
        sums.append(jnp.sum(jnp.sum(terms, axis=1, keepdims=True), axis=0, keepdims=True))
    line = lax.broadcasted_iota(jnp.int32, (8, 128), 0)
    board = jnp.zeros((8, 128), jnp.float32)
    for e, value in enumerate(sums):
        board = jnp.where(line == e, value, board)
    tiles[t] = board
    for k in range(1, width):
        send_tile(k).start()
    fetch(1)
    spread(3)

    @pl.loop(0, D // 256)
    def _(d):
        lines = pl.ds(pl.multiple_of(d * 256, 256), 256)
        total = nt(ob[0], gw_v[lines, :]) + nt(ob[1], uw_v[lines, :])
        partial[:, lines] = total.astype(jnp.bfloat16)

    for j in range(1, planes):
        if j > 1:
            spread(j + 2)
        load(j).wait()
        part(j, 0)
        if j == 1:
            for k in range(1, width):
                take_tile(k).wait_recv()
            norms[z] = jnp.sum(tiles[...], axis=0)
            for i in range(1, planes):
                send_norm(i).start()
        hand_on(j + 1)
        part(j, 1)
        hand_across(j + 1)
        if j == planes - 2:
            for k in range(1, width):
                send_rows(k).start()
        part(j, 2)
        fetch(j + 1)
        part(j, 3)
        cut(j)

    mine = pl.ds(pl.multiple_of(t * rows, rows), rows)
    total = partial[mine, :].astype(jnp.float32)
    for k in range(1, width):
        send_rows(k).wait_recv()
        total = total + landed[k].astype(jnp.float32)
    input_grad[...] = total.astype(jnp.bfloat16)
    for i in range(1, planes):
        take_norm(i).wait_recv()
    clip_level = math.sqrt(SEQ * D * (FF // 2 + D))
    for p in range(planes):
        factor = math.sqrt(D * FF) / jnp.maximum(clip_level, jnp.sqrt(norms[p]))
        for e in range(many // SEQ):
            at = slice(e * SEQ, (e + 1) * SEQ)
            for a in range(2):
                scaled[a][p, at, :] = (
                    scaled[a][p, at, :].astype(jnp.float32) * factor[e : e + 1, :1]
                ).astype(jnp.bfloat16)

    for j in range(1, planes):
        to_z(j).wait_send()
        send_norm(j).wait_send()
    for k in range(1, width):
        send_tile(k).wait_send()
        send_rows(k).wait_send()
    for j in range(planes):
        for k in direct:
            to_peer(j, k).wait_send()
        if folded:
            for f in range(2):
                to_across(j, f).wait_send()
        for k in range(chips):
            to_sibling(j, k).wait_send()
    if n_tiles == 1:
        for copy in out_copies(planes - 1, 0, slice(None)):
            copy.wait()
    else:
        @pl.loop(0, n_tiles)
        def _(n):
            for copy in out_copies(planes - 1, n, pl.ds(pl.multiple_of(n * step, step), step)):
                copy.wait()


def body(planes, width, tokens, cotangent, gate_weight, up_weight, down_weight):
    rows, units = tokens.shape[0], gate_weight.shape[1]
    many, chips = rows * width, width // 2
    tiles = units // 256 if units % 256 == 0 else 1
    half = jnp.bfloat16
    anywhere = pl.BlockSpec(memory_space=pl.ANY)
    inside = pl.BlockSpec(memory_space=pltpu.VMEM)
    dma = pltpu.SemaphoreType.DMA
    produced = jax.ShapeDtypeStruct((planes, many, units), half)
    sliced = jax.ShapeDtypeStruct((planes, many, D // planes), half)
    _, gate, up, hidden, scaled_in, scaled_cot, input_grad = pl.pallas_call(
        functools.partial(kernel, planes, width),
        out_shape=(
            jax.ShapeDtypeStruct((2, planes, many, D), half),
            produced, produced, produced,
            sliced, sliced,
            jax.ShapeDtypeStruct((rows, D), half),
        ),
        in_specs=[anywhere] * 4,
        out_specs=(anywhere,) * 4 + (inside,) * 3,
        scratch_shapes=[
            pltpu.VMEM((D, units), half),
            pltpu.VMEM((D, units), half),
            pltpu.VMEM((units, D), half),
            pltpu.VMEM((2, 2, many, D), half),
            pltpu.VMEM((3, many, units), half),
            pltpu.VMEM((many, D), half),
            pltpu.VMEM((width, rows, D), half),
            pltpu.VMEM((width, 8, 128), jnp.float32),
            pltpu.VMEM((planes, 8, 128), jnp.float32),
            dma((3,)), dma, dma((2,)), dma((3, tiles)),
            dma((planes,)), dma((planes,)),
            dma((planes, chips)), dma((planes, chips)),
            dma((planes, chips)), dma((planes, chips)),
            dma((width,)), dma((width,)),
            dma((width,)), dma((width,)),
            dma((planes,)), dma((planes,)),
            dma((planes, 2)), dma((planes, 2)),
        ],
        compiler_params=pltpu.CompilerParams(
            collective_id=0, has_side_effects=True, vmem_limit_bytes=63 * 1024 * 1024
        ),
    )(jnp.stack([tokens, cotangent]), gate_weight, up_weight, down_weight)

    scaled = [a.reshape(planes * many, D // planes) for a in (scaled_in, scaled_cot)]

    def first(a, b):
        return lax.dot_general(a, b, (((0,), (0,)), ((), ())), preferred_element_type=jnp.float32)

    grad_gate = first(scaled[0], gate.reshape(planes * many, units))
    grad_up = first(scaled[0], up.reshape(planes * many, units))
    grad_down = first(hidden.reshape(planes * many, units), scaled[1])
    return (input_grad, grad_gate, grad_up, grad_down)


def solution(mesh):
    placed = (
        P(("dp", "tensor"), None),
        P(("dp", "tensor"), None),
        P(None, "tensor"),
        P(None, "tensor"),
        P("tensor", None),
    )
    return jax.shard_map(
        functools.partial(body, mesh.shape["dp"], mesh.shape["tensor"]),
        mesh=mesh,
        in_specs=placed,
        out_specs=(
            P(("dp", "tensor"), None),
            P("dp", "tensor"),
            P("dp", "tensor"),
            P("tensor", "dp"),
        ),
        check_vma=False,
    )
```
